32 devices in a mesh: groups: 2 (over y), fsdp: 8 (over z, x), batch: 2 (over core).
Axes of the slice: x: 2, y: 2, z: 4, core: 2. Of those that a mesh axis runs over, the one named last changes fastest.
Arguments:
- activations: bfloat16 [2, 2048, 8192], P('batch', ('groups', 'fsdp')), parts along dimension 1, may hold values from -6 to 6
- cotangent: bfloat16 [2, 2048, 8192], P('batch', ('groups', 'fsdp')), parts along dimension 1, may hold values from -6 to 6
- adapter: bfloat16 [2, 8192, 128], P(None, 'fsdp'), may hold values from -0.0625 to 0.0625
- lengths: int32 [2, 4], P(None, 'groups'), parts along dimension 1, may hold values from 128 to 512, as said below
- layout: int32 [2, 16], P(None, 'groups'), parts along dimension 1, may hold values from 0 to 7, each once within a row
- feature_signs: int32 [2, 8192], replicated, may hold values from 0 to 1
- rank_signs: int32 [2, 128], replicated, may hold values from 0 to 1
- hadamard_rows: int32 [2, 8192], replicated, may hold values from 0 to 8191, each once within a row
- entry_pick: int32 [2, 4096], replicated, may hold values from 0 to 131071
- val_feats: float32 [512, 8192], P('groups', 'fsdp'), parts along dimension 0, may hold values from -600 to 600
Outputs:
- similarity: float32 [2, 4, 256], P('batch', 'groups'), parts along dimension 1
The draws below stay inside these ranges and needn't reach their ends.
There are 2 independent parts, one for each index of `groups`. The reference program is written for one: setup_inputs(seed, part) draws one part's arguments, and reference() takes and returns one part's arrays. A program takes and returns all parts, laid end to end along the dimension named above; an argument that names none is the same for every part. Nothing has to cross between parts.
Inputs may be any that keep to these rules, and one draw needn't show every extreme that they name: `lengths`: every example has at least 128 real tokens, and some example of each draw has 512. Each row is a permutation; index i of fsdp holds block s % 4 of example s // 4, s = layout[m, i]. `hadamard_rows`: each row is a permutation. `entry_pick`: row 0 indexes the row-major 1024 x 128 grid_a, row 1 the row-major 128 x 1024 grid_b.
All inputs are finite; a program needn't handle non-finite values.
Results may differ from the reference program's by a relative error of at most 0.0003.
Values may be sent and summed in bfloat16 or wider, within the bound.
A program may use at most 64 MiB of HBM per device.

```python
import math
import jax
import jax.numpy as jnp
from jax import lax

D = 8192
R = 128
K = 8192
CAND = 1024
TOK_DEV = 128
EX_LEN = 512
VAL = 256
MICRO = 2
TOKENS = 1024
EXAMPLES = 2
BLOCKS = 4
N_FSDP = 8


def draw_lengths(key, part):
    key = jax.random.fold_in(key, 11)
    key_raw, key_pick = jax.random.split(key)
    raw_len = jax.random.randint(key_raw, (MICRO * EXAMPLES,), EX_LEN // 4, EX_LEN + 1, dtype=jnp.int32)
    chosen = jax.random.randint(key_pick, (), 0, MICRO * EXAMPLES, dtype=jnp.int32)
    filled = jnp.where(jnp.arange(MICRO * EXAMPLES, dtype=jnp.int32) == chosen, EX_LEN, raw_len)
    return filled.reshape(MICRO, EXAMPLES).astype(jnp.int32)


def draw_val_feats(key, part):
    key = jax.random.fold_in(key, 23)
    key_base, key_rows, key_cols = jax.random.split(key, 3)
    row_scale = jnp.exp(jax.random.uniform(key_rows, (VAL, 1), jnp.float32) * math.log(10.0))
    col_scale = jnp.exp(jax.random.uniform(key_cols, (1, K), jnp.float32) * math.log(10.0))
    base_vals = jnp.clip(jax.random.normal(key_base, (VAL, K), jnp.float32), -6.0, 6.0)
    return (base_vals * row_scale * col_scale).astype(jnp.float32)


def with_ends(result, stream_key, smallest, top_value):
    dims = result.shape
    place = [jax.random.randint(jax.random.fold_in(stream_key, axis), (), 0, dims[axis]) for axis in range(len(dims))]
    result = result.at[tuple(place)].set(smallest)
    longest = dims.index(max(dims))
    place[longest] = (place[longest] + 1) % dims[longest]
    return result.at[tuple(place)].set(top_value)


def shard_levels(key, dims, cuts, low, top_value):
    def one(dim, shards_of):
        steps = jax.random.uniform(jax.random.fold_in(jax.random.fold_in(key, 6), dim), (shards_of,), jnp.float32, low / len(cuts), top_value / len(cuts))
        return jnp.repeat(jnp.exp(steps), dims[dim] // shards_of).reshape((-1,) + (1,) * (len(dims) - dim - 1))

    loudness = one(*cuts[0])
    for cut in cuts[1:]:
        loudness = loudness * one(*cut)
    return loudness


def scatter_about(key, shape, width, most, pieces=(), held_as=jnp.bfloat16):
    array = width * jax.random.normal(key, shape, jnp.float32)
    if pieces:
        array = array * shard_levels(key, shape, pieces, -0.22, 0.18)
    return jnp.clip(array, -most, most).astype(held_as)


def setup_inputs(seed: int = 0, part: int = 0) -> dict:
    key_of = jax.random.split(jax.random.key(seed), 11)
    part_splits = jax.random.split(jax.random.fold_in(key_of[10], part), 11)
    return {
        "activations": scatter_about(part_splits[0], (MICRO, TOKENS, D), 1.0, 6.0, ((0, 2), (1, 8))),
        "cotangent": scatter_about(part_splits[1], (MICRO, TOKENS, D), 1.0, 6.0, ((0, 2), (1, 8))),
        "adapter": scatter_about(key_of[2], (2, D, R), D ** -0.5, 0.0625, ((1, 8),)),
        "lengths": draw_lengths(jax.random.fold_in(jax.random.fold_in(key_of[10], part), 71), part),
        "layout": jax.vmap(lambda own: jax.random.permutation(own, N_FSDP))(jax.random.split(part_splits[4], MICRO)).reshape((MICRO, N_FSDP)).astype(jnp.int32),
        "feature_signs": with_ends(jax.random.randint(key_of[5], (2, D), 0, 2), jax.random.fold_in(key_of[5], 1), 0, 1).astype(jnp.int32),
        "rank_signs": with_ends(jax.random.randint(key_of[6], (2, R), 0, 2), jax.random.fold_in(key_of[6], 1), 0, 1).astype(jnp.int32),
        "hadamard_rows": jax.vmap(lambda own: jax.random.permutation(own, D))(jax.random.split(key_of[7], 2)).reshape((2, D)).astype(jnp.int32),
        "entry_pick": with_ends(jax.random.randint(key_of[8], (2, K // 2), 0, CAND * R), jax.random.fold_in(key_of[8], 1), 0, (CAND * R) - 1).astype(jnp.int32),
        "val_feats": draw_val_feats(jax.random.fold_in(jax.random.fold_in(key_of[10], part), 71), part),
    }


def hadamard_last(values):
    length = values.shape[-1]
    stride = 1
    while stride < length:
        shaped = values.reshape(values.shape[:-1] + (length // (2 * stride), 2, stride))
        upper_half = shaped[..., 0, :]
        lower_half = shaped[..., 1, :]
        values = jnp.stack([upper_half + lower_half, upper_half - lower_half], axis=-2)
        values = values.reshape(shaped.shape[:-3] + (length,))
        stride = stride * 2
    return values

def reference(activations, cotangent, adapter, lengths, layout, feature_signs, rank_signs, hadamard_rows, entry_pick, val_feats):
    signs_in = (1 - 2 * feature_signs[0]).astype(jnp.float32)
    signs_out = (1 - 2 * feature_signs[1]).astype(jnp.float32)
    rank_a = (1 - 2 * rank_signs[0]).astype(jnp.float32)
    rank_b = (1 - 2 * rank_signs[1]).astype(jnp.float32)
    rows_a = hadamard_rows[0, :CAND]
    rows_b = hadamard_rows[1, :CAND]
    pick_a = entry_pick[0]
    pick_b = entry_pick[1]
    example_of = layout // BLOCKS
    block_in = layout % BLOCKS
    length_of = jnp.take_along_axis(lengths, example_of, axis=1)
    act_blocks = activations.reshape(MICRO * N_FSDP, TOK_DEV, D)
    cot_blocks = cotangent.reshape(MICRO * N_FSDP, TOK_DEV, D)
    starts = (block_in * TOK_DEV).reshape(-1).astype(jnp.int32)
    limits = length_of.reshape(-1).astype(jnp.int32)
    scale_wide = 1.0 / math.sqrt(D)
    scale_rank = 1.0 / math.sqrt(R)

    def one_block(packed):
        act_block, cot_block, start_pos, limit_len = packed
        position = start_pos + jnp.arange(TOK_DEV, dtype=jnp.int32)
        weight = (position < limit_len).astype(jnp.float32)[:, None]
        reduced = jnp.dot(act_block, adapter[0], preferred_element_type=jnp.float32)
        backward = jnp.dot(cot_block, adapter[1], preferred_element_type=jnp.float32)
        left_a = hadamard_last(act_block.astype(jnp.float32) * signs_in)[:, rows_a] * scale_wide
        right_a = hadamard_last(backward * rank_a) * scale_rank * weight
        left_b = hadamard_last(reduced * rank_b) * scale_rank * weight
        right_b = hadamard_last(cot_block.astype(jnp.float32) * signs_out)[:, rows_b] * scale_wide
        grid_a = jnp.dot(left_a.T, right_a, precision=lax.Precision.HIGHEST, preferred_element_type=jnp.float32)
        grid_b = jnp.dot(left_b.T, right_b, precision=lax.Precision.HIGHEST, preferred_element_type=jnp.float32)
        return jnp.concatenate([grid_a.reshape(-1)[pick_a], grid_b.reshape(-1)[pick_b]])
    partial_feats = lax.map(one_block, (act_blocks, cot_blocks, starts, limits))
    partial_feats = partial_feats.reshape(MICRO, N_FSDP, K)
    owners = (example_of[:, None, :] == jnp.arange(EXAMPLES, dtype=jnp.int32)[None, :, None]).astype(jnp.float32)
    features = jnp.einsum('men,mnk->mek', owners, partial_feats, precision=lax.Precision.HIGHEST)
    dots = jnp.einsum('mek,vk->mev', features, val_feats.astype(jnp.float32), precision=lax.Precision.HIGHEST)
    feat_sq = lax.optimization_barrier(jnp.sum(features * features, axis=-1))
    val_sq = lax.optimization_barrier(jnp.sum(val_feats * val_feats, axis=-1))
    similarity = math.sqrt(K) * dots * lax.rsqrt(feat_sq[:, :, None] + 1e-06) * lax.rsqrt(val_sq[None, None, :] + 1e-06)
    return similarity
```

```python
import math

import jax
import jax.numpy as jnp
from jax import lax
from jax.experimental import pallas as pl
from jax.experimental.pallas import tpu as pltpu
from jax.sharding import PartitionSpec as P

K = 8192
CAND = 1024
EX_LEN = 512


def bit_parity(values):
    counted = jnp.zeros_like(values)
    for shift_amount in range(16):
        counted = counted + jnp.bitwise_and(jnp.right_shift(values, shift_amount), 1)
    return jnp.bitwise_and(counted, 1)


def parity_table(left_bits, right_bits):
    anded = jnp.bitwise_and(left_bits[:, None], right_bits[None, :])
    return 1 - 2 * bit_parity(anded)


def project_rows(inputs, rows_chosen):
    tok_count, feature_width = inputs.shape
    low_size = min(feature_width, 1024)
    high_count = feature_width // low_size
    low_bits = jnp.arange(low_size, dtype=jnp.int32)
    base_table = parity_table(low_bits, rows_chosen).astype(jnp.bfloat16)
    high_bits = jnp.arange(high_count, dtype=jnp.int32) * low_size
    signs_high = parity_table(high_bits, rows_chosen).astype(jnp.float32)
    pieces = inputs.reshape(tok_count, high_count, low_size)
    partial_value = jnp.einsum(
        "thd,dk->thk", pieces, base_table, preferred_element_type=jnp.float32
    )
    return jnp.sum(partial_value * signs_high[None, :, :], axis=1) / math.sqrt(feature_width)


def rank_mix(values, signs):
    rank_size = values.shape[1]
    rank_bits = jnp.arange(rank_size, dtype=jnp.int32)
    table = parity_table(rank_bits, rank_bits).astype(jnp.float32)
    mixed = jnp.dot(
        values * signs, table, precision=lax.Precision.HIGHEST, preferred_element_type=jnp.float32
    )
    return mixed / math.sqrt(rank_size)


def per_device_any_size(
    activations,
    cotangent,
    adapter,
    lengths,
    layout,
    feature_signs,
    rank_signs,
    hadamard_rows,
    entry_pick,
    val_feats,
):
    micro_index = lax.axis_index("batch")
    member = lax.axis_index("fsdp")
    tok_count = activations.shape[1]
    block_count = EX_LEN // tok_count
    example_total = lengths.shape[1]
    slot_row = lax.dynamic_index_in_dim(layout, micro_index, 0, keepdims=False)
    my_slot = lax.dynamic_index_in_dim(slot_row, member, 0, keepdims=False)
    my_example = my_slot // block_count
    length_row = lax.dynamic_index_in_dim(lengths, micro_index, 0, keepdims=False)
    my_length = lax.dynamic_index_in_dim(length_row, my_example, 0, keepdims=False)
    position = my_slot % block_count * tok_count + jnp.arange(tok_count, dtype=jnp.int32)
    weight = (position < my_length).astype(jnp.float32)[:, None]
    inputs = activations[0]
    grads = cotangent[0]
    piece = lax.all_gather(adapter, "fsdp", axis=1, tiled=True)
    reduced = jnp.dot(inputs, piece[0], preferred_element_type=jnp.float32)
    backward = jnp.dot(grads, piece[1], preferred_element_type=jnp.float32)
    signs_in = (1 - 2 * feature_signs[0]).astype(jnp.bfloat16)
    signs_out = (1 - 2 * feature_signs[1]).astype(jnp.bfloat16)
    rank_a = (1 - 2 * rank_signs[0]).astype(jnp.float32)
    rank_b = (1 - 2 * rank_signs[1]).astype(jnp.float32)
    left_a = project_rows(inputs * signs_in[None, :], hadamard_rows[0, :CAND])
    right_b = project_rows(grads * signs_out[None, :], hadamard_rows[1, :CAND])
    right_a = rank_mix(backward, rank_a) * weight
    left_b = rank_mix(reduced, rank_b) * weight
    grid_a = jnp.dot(
        left_a.T, right_a, precision=lax.Precision.HIGHEST, preferred_element_type=jnp.float32
    )
    grid_b = jnp.dot(
        left_b.T, right_b, precision=lax.Precision.HIGHEST, preferred_element_type=jnp.float32
    )
    partial_feats = jnp.concatenate(
        [grid_a.reshape(-1)[entry_pick[0]], grid_b.reshape(-1)[entry_pick[1]]]
    )
    example_ids = jnp.arange(example_total, dtype=jnp.int32)
    mine = (example_ids == my_example).astype(jnp.float32)
    term = mine[:, None] * partial_feats[None, :]
    feat_slice = lax.psum_scatter(term, "fsdp", scatter_dimension=1, tiled=True)
    dots = jnp.dot(
        feat_slice, val_feats.T, precision=lax.Precision.HIGHEST, preferred_element_type=jnp.float32
    )
    feat_sq = jnp.sum(feat_slice * feat_slice, axis=1)
    val_sq = jnp.sum(val_feats * val_feats, axis=1)
    dots, feat_sq, val_sq = lax.psum((dots, feat_sq, val_sq), "fsdp")
    similarity = (
        math.sqrt(K)
        * dots
        * lax.rsqrt(feat_sq[:, None] + 1e-06)
        * lax.rsqrt(val_sq[None, :] + 1e-06)
    )
    return similarity[None]


MESH = pl.DeviceIdType.MESH
F32 = jnp.float32
BF16 = jnp.bfloat16
D_MODEL = 8192
RANK = 128
LOW = 1024
HIGH = D_MODEL // LOW
TOK = 128
MEMBERS = 8
SHARD = D_MODEL // MEMBERS
HALF = K // 2
VALS = 256
SLICE = K // MEMBERS
PLANE_ROWS = 640
CROSS_ROWS = SHARD - PLANE_ROWS


def sign_rows(row, bit):
    signs = (1 - 2 * jnp.bitwise_and(jnp.right_shift(row, bit), 1)).astype(F32)
    return jnp.broadcast_to(signs, (16, row.shape[1])).astype(BF16)


def fill_signs(table_ref, row, bits):
    width = row.shape[1]
    index = lax.broadcasted_iota(jnp.int32, (16, width), 0)
    both = jnp.bitwise_and(index, jnp.broadcast_to(row, (16, width)))
    both = jnp.bitwise_xor(both, jnp.right_shift(both, 2))
    both = jnp.bitwise_xor(both, jnp.right_shift(both, 1))
    table_ref[0:16, :] = (1 - 2 * jnp.bitwise_and(both, 1)).astype(F32).astype(BF16)
    for bit in range(4, bits):
        flip = sign_rows(row, bit)
        span = 1 << bit
        for at in range(0, span, 16):
            table_ref[span + at : span + at + 16, :] = table_ref[at : at + 16, :] * flip


def split_rows(values):
    top = values.astype(BF16)
    rest = (values - top.astype(F32)).astype(BF16)
    return jnp.concatenate([top, rest], axis=0)


def dot_t(left, right):
    return lax.dot_general(
        left, right, (((1,), (1,)), ((), ())), preferred_element_type=F32
    )


def kernel(
    lengths_ref,
    layout_ref,
    signs_ref,
    rank_ref,
    rows_ref,
    pick_ref,
    act_hbm,
    cot_hbm,
    adapter_hbm,
    val_hbm,
    out_ref,
    act_ref,
    cot_ref,
    val_ref,
    gathered,
    x_ref,
    t_ref,
    left_ref,
    sel_a,
    sel_b,
    mix_a,
    mix_b,
    val_parts,
    val_sq,
    feat_out,
    feat_in,
    dots_out,
    dots_in,
    local_sem,
    z_send,
    z_recv,
    x_send,
    x_recv,
    y_send,
    y_recv,
    ca_send,
    ca_recv,
    cb_send,
    cb_recv,
    f_send,
    f_recv,
    d_send,
    d_recv,
):
    group = lax.axis_index("groups")
    member = lax.axis_index("fsdp")
    core = lax.axis_index("batch")
    col = member % 2
    depth = member // 2
    mates = [
        depth,
        depth + 1 - 2 * (depth % 2),
        (depth + 2) % 4,
        3 - depth,
    ]
    other_group = {"groups": 1 - group}
    other_core = {"batch": 1 - core}
    across = {"fsdp": depth * 2 + 1 - col}

    loads = [
        pltpu.make_async_copy(act_hbm.at[0], act_ref, local_sem.at[0]),
        pltpu.make_async_copy(cot_hbm.at[0], cot_ref, local_sem.at[1]),
        pltpu.make_async_copy(val_hbm, val_ref, local_sem.at[2]),
        pltpu.make_async_copy(adapter_hbm.at[0], gathered.at[0, member], local_sem.at[3]),
        pltpu.make_async_copy(adapter_hbm.at[1], gathered.at[1, member], local_sem.at[4]),
    ]
    for load in loads:
        load.start()

    barrier = pltpu.get_barrier_semaphore()
    for step in range(1, MEMBERS):
        pl.semaphore_signal(
            barrier, inc=1, device_id={"fsdp": (member + step) % MEMBERS}, device_id_type=MESH
        )
    pl.semaphore_signal(barrier, inc=1, device_id=other_group, device_id_type=MESH)
    pl.semaphore_signal(barrier, inc=1, device_id=other_core, device_id_type=MESH)
    pl.semaphore_wait(barrier, MEMBERS + 1)

    plane = pl.ds(pl.multiple_of(group * CROSS_ROWS, 128), PLANE_ROWS)
    cross_out = pl.ds(pl.multiple_of(group * PLANE_ROWS, 128), CROSS_ROWS)
    cross_in = pl.ds(pl.multiple_of((1 - group) * PLANE_ROWS, 128), CROSS_ROWS)
    own = adapter_hbm.at[core, plane]

    def remote(src, dst, send, recv, where):
        return pltpu.make_async_remote_copy(
            src_ref=src,
            dst_ref=dst,
            send_sem=send,
            recv_sem=recv,
            device_id=where,
            device_id_type=MESH,
        )

    sent = []

    def go(copy):
        copy.start()
        sent.append(copy)

    home = gathered.at[core, member, plane]
    go(remote(own, home, x_send.at[0], x_recv.at[0], across))
    for k in (3, 2, 1):
        go(remote(own, home, z_send.at[k], z_recv.at[k], {"fsdp": mates[k] * 2 + col}))

    order = [("x", 0), ("z", 1), ("x", 1), ("z", 3), ("x", 3), ("z", 2), ("x", 2)]
    shard_of = [
        mates[k] * 2 + (col if kind == "z" else 1 - col) for kind, k in order
    ]

    def receive(place):
        kind, k = order[place]
        shard = shard_of[place]
        block = gathered.at[core, shard, plane]
        sems = (z_send, z_recv) if kind == "z" else (x_send, x_recv)
        remote(block, block, sems[0].at[k], sems[1].at[k], across).wait_recv()
        if kind == "z":
            go(remote(block, block, x_send.at[k], x_recv.at[k], across))
        part = gathered.at[core, shard, cross_out]
        go(remote(part, part, y_send.at[place], y_recv.at[place], other_group))
        go(remote(block, block, ca_send.at[place], ca_recv.at[place], other_core))

    def receive_cross(place):
        part = gathered.at[core, shard_of[place], cross_in]
        remote(part, part, y_send.at[place], y_recv.at[place], other_group).wait_recv()
        go(remote(part, part, cb_send.at[place], cb_recv.at[place], other_core))

    def receive_core(place):
        block = gathered.at[1 - core, shard_of[place], plane]
        part = gathered.at[1 - core, shard_of[place], cross_in]
        remote(block, block, ca_send.at[place], ca_recv.at[place], other_core).wait_recv()
        remote(part, part, cb_send.at[place], cb_recv.at[place], other_core).wait_recv()

    def fill_inputs(which, in_ref):
        for high in range(HIGH):
            lanes = slice(high * LOW, (high + 1) * LOW)
            flip = sign_rows(signs_ref[which : which + 1, lanes], 0)
            for at in range(0, TOK, 16):
                x_ref[high * TOK + at : high * TOK + at + 16, :] = (
                    in_ref[at : at + 16, lanes] * flip
                )

    def project(which):
        def tile(n, carry):
            lanes = pl.ds(pl.multiple_of(n * 256, 256), 256)
            parts = jnp.dot(x_ref[...], t_ref[:, lanes], preferred_element_type=F32)
            row = rows_ref[which : which + 1, lanes]
            level = [parts[h * TOK : (h + 1) * TOK] for h in range(HIGH)]
            for bit in range(10, 13):
                flip = (1 - 2 * jnp.bitwise_and(jnp.right_shift(row, bit), 1)).astype(F32)
                level = [
                    level[2 * i] + level[2 * i + 1] * flip for i in range(len(level) // 2)
                ]
            left_ref[:, lanes] = split_rows(level[0])
            return carry

        lax.fori_loop(0, CAND // 256, tile, 0)

    def row_index(which, lanes):
        picked = pick_ref[which : which + 1, lanes]
        if which == 0:
            return jnp.right_shift(picked, 7)
        return jnp.bitwise_and(picked, CAND - 1)

    def rank_index(which):
        picked = pick_ref[which : which + 1, :]
        if which == 0:
            return jnp.bitwise_and(picked, RANK - 1)
        return jnp.right_shift(picked, 10)

    def select(which, sel_ref, begin, end):
        def tile(n, carry):
            lanes = pl.ds(pl.multiple_of(n * 256, 256), 256)
            wanted = row_index(which, lanes)
            index = lax.broadcasted_iota(jnp.int32, (CAND, 256), 0)
            hot = jnp.where(index == wanted, 1.0, 0.0).astype(BF16)
            both = jnp.dot(left_ref[...], hot, preferred_element_type=F32)
            sel_ref[:, lanes] = both[:TOK] + both[TOK:]
            return carry

        lax.fori_loop(begin, end, tile, 0)

    def prepare_scores():
        values = val_ref[...]
        val_parts[...] = split_rows(values)
        squares = split_rows(values * values)
        sums = dot_t(jnp.ones((16, SLICE), BF16), squares)
        val_sq[...] = sums[0:8, :VALS] + sums[0:8, VALS:]

    loads[0].wait()
    fill_signs(t_ref, rows_ref[0:1, 0:CAND], 10)
    fill_inputs(0, act_ref)
    project(0)
    receive(0)
    receive(1)
    select(0, sel_a, 0, 8)
    receive(2)
    select(0, sel_a, 8, 16)
    receive(3)
    receive_cross(0)
    receive_cross(1)
    loads[1].wait()
    fill_signs(t_ref, rows_ref[1:2, 0:CAND], 10)
    fill_inputs(1, cot_ref)
    receive(4)
    receive_cross(2)
    project(1)
    receive(5)
    receive_cross(3)
    select(1, sel_b, 0, 8)
    receive(6)
    receive_cross(4)
    select(1, sel_b, 8, 16)
    receive_cross(5)
    fill_signs(mix_a, rank_index(0), 7)
    fill_signs(mix_b, rank_index(1), 7)
    receive_cross(6)
    loads[2].wait()
    prepare_scores()
    loads[3].wait()
    loads[4].wait()

    def both_products(shard):
        lanes = pl.ds(pl.multiple_of(shard * SHARD, SHARD), SHARD)
        return (
            jnp.dot(act_ref[:, lanes], gathered[0, shard], preferred_element_type=F32),
            jnp.dot(cot_ref[:, lanes], gathered[1, shard], preferred_element_type=F32),
        )

    reduced, backward = both_products(member)
    for place in range(MEMBERS - 1):
        receive_core(place)
        more_r, more_b = both_products(shard_of[place])
        reduced = reduced + more_r
        backward = backward + more_b

    slot = layout_ref[core, member]
    blocks = EX_LEN // TOK
    example = slot // blocks
    length = jnp.int32(0)
    for e in range(lengths_ref.shape[1]):
        length = jnp.where(example == e, lengths_ref[core, e], length)
    position = slot % blocks * TOK + lax.broadcasted_iota(jnp.int32, (TOK, RANK), 0)
    weight = jnp.where(position < length, 1.0, 0.0)
    rank_flip = (1 - 2 * rank_ref[...]).astype(F32)
    mixed_a = split_rows(backward * rank_flip[0:1] * weight)
    mixed_b = split_rows(reduced * rank_flip[1:2] * weight)
    scale = 1.0 / math.sqrt(D_MODEL * RANK)
    for n in range(MEMBERS):
        mixed, mix, sel = (mixed_a, mix_a, sel_a) if n < MEMBERS // 2 else (mixed_b, mix_b, sel_b)
        lanes = slice(n % (MEMBERS // 2) * SLICE, (n % (MEMBERS // 2) + 1) * SLICE)
        both = jnp.dot(mixed, mix[:, lanes], preferred_element_type=F32)
        terms = sel[:, lanes] * (both[:TOK] + both[TOK:])
        feat_out[n] = jnp.sum(terms, axis=0, keepdims=True) * scale

    feat_in[member] = feat_out[member]
    for step in range(1, MEMBERS):
        to = (member + step) % MEMBERS
        go(
            remote(
                feat_out.at[to], feat_in.at[member], f_send.at[step], f_recv.at[step], {"fsdp": to}
            )
        )
    for step in range(1, MEMBERS):
        source = (member + MEMBERS - step) % MEMBERS
        remote(
            feat_out.at[source], feat_in.at[source], f_send.at[step], f_recv.at[step],
            {"fsdp": source},
        ).wait_recv()

    examples = lengths_ref.shape[1]
    totals = [jnp.zeros((1, SLICE), F32) for _ in range(examples)]
    for n in range(MEMBERS):
        owner = layout_ref[core, n] // blocks
        piece = feat_in[n]
        for e in range(examples):
            totals[e] = totals[e] + piece * jnp.where(owner == e, 1.0, 0.0)
    row_at = lax.broadcasted_iota(jnp.int32, (8, SLICE), 0)
    feats = jnp.zeros((8, SLICE), F32)
    for e in range(examples):
        feats = jnp.where(row_at == e, jnp.broadcast_to(totals[e], (8, SLICE)), feats)
    products = dot_t(split_rows(feats), val_parts[...])
    dots = products[0:8, :VALS] + (products[8:16, :VALS] + products[0:8, VALS:])
    feat_sq = jnp.sum(feats * feats, axis=1, keepdims=True)
    at = lax.broadcasted_iota(jnp.int32, (8, VALS), 0)
    dots_out[:, 0:VALS] = jnp.where(at == examples, val_sq[...], dots)
    dots_out[:, VALS:] = jnp.broadcast_to(feat_sq, (8, RANK))
    dots_in[member] = dots_out[...]
    for step in range(1, MEMBERS):
        to = (member + step) % MEMBERS
        go(remote(dots_out, dots_in.at[member], d_send.at[step], d_recv.at[step], {"fsdp": to}))
    for step in range(1, MEMBERS):
        source = (member + MEMBERS - step) % MEMBERS
        remote(
            dots_out, dots_in.at[source], d_send.at[step], d_recv.at[step], {"fsdp": source}
        ).wait_recv()
    total = dots_in[0]
    for n in range(1, MEMBERS):
        total = total + dots_in[n]
    out_ref[0] = (
        math.sqrt(K)
        * total[0:examples, 0:VALS]
        * lax.rsqrt(total[0:examples, VALS : VALS + 1] + 1e-06)
        * lax.rsqrt(total[examples : examples + 1, 0:VALS] + 1e-06)
    )
    for copy in sent:
        copy.wait_send()


def per_device(
    activations,
    cotangent,
    adapter,
    lengths,
    layout,
    feature_signs,
    rank_signs,
    hadamard_rows,
    entry_pick,
    val_feats,
):
    examples = lengths.shape[1]
    smem = pl.BlockSpec(memory_space=pltpu.SMEM)
    vmem = pl.BlockSpec(memory_space=pltpu.VMEM)
    hbm = pl.BlockSpec(memory_space=pl.ANY)
    dma = pltpu.SemaphoreType.DMA
    return pl.pallas_call(
        kernel,
        out_shape=jax.ShapeDtypeStruct((1, examples, VALS), F32),
        in_specs=[smem] * 2 + [vmem] * 4 + [hbm] * 4,
        out_specs=vmem,
        scratch_shapes=[
            pltpu.VMEM((TOK, D_MODEL), BF16),
            pltpu.VMEM((TOK, D_MODEL), BF16),
            pltpu.VMEM((VALS, SLICE), F32),
            pltpu.VMEM((2, MEMBERS, SHARD, RANK), BF16),
            pltpu.VMEM((HIGH * TOK, LOW), BF16),
            pltpu.VMEM((LOW, CAND), BF16),
            pltpu.VMEM((2 * TOK, CAND), BF16),
            pltpu.VMEM((TOK, HALF), F32),
            pltpu.VMEM((TOK, HALF), F32),
            pltpu.VMEM((RANK, HALF), BF16),
            pltpu.VMEM((RANK, HALF), BF16),
            pltpu.VMEM((2 * VALS, SLICE), BF16),
            pltpu.VMEM((8, VALS), F32),
            pltpu.VMEM((MEMBERS, 1, SLICE), F32),
            pltpu.VMEM((MEMBERS, 1, SLICE), F32),
            pltpu.VMEM((8, VALS + RANK), F32),
            pltpu.VMEM((MEMBERS, 8, VALS + RANK), F32),
            dma((5,)),
        ]
        + [dma((4,))] * 4
        + [dma((MEMBERS,))] * 10,
        compiler_params=pltpu.CompilerParams(
            collective_id=0, has_side_effects=True, vmem_limit_bytes=48 * 1024 * 1024
        ),
        cost_estimate=pl.CostEstimate(
            flops=10_000_000_000, bytes_accessed=8_000_000, transcendentals=0
        ),
    )(
        lengths,
        layout,
        feature_signs,
        rank_signs,
        hadamard_rows,
        entry_pick,
        activations,
        cotangent,
        adapter,
        val_feats,
    )


def solution(mesh):
    fits = mesh.shape["fsdp"] == MEMBERS and mesh.shape["batch"] == 2 and mesh.shape["groups"] == 2
    return jax.shard_map(
        per_device if fits else per_device_any_size,
        mesh=mesh,
        in_specs=(
            P("batch", ("groups", "fsdp"), None),
            P("batch", ("groups", "fsdp"), None),
            P(None, "fsdp", None),
            P(None, "groups"),
            P(None, "groups"),
            P(),
            P(),
            P(),
            P(),
            P("groups", "fsdp"),
        ),
        out_specs=P("batch", "groups", None),
        check_vma=False,
    )
```

```python
import math

import jax
import jax.numpy as jnp
from jax import lax
from jax.experimental import pallas as pl
from jax.experimental.pallas import tpu as pltpu
from jax.sharding import PartitionSpec as P

K = 8192
CAND = 1024
EX_LEN = 512


def bit_parity(values):
    counted = jnp.zeros_like(values)
    for shift_amount in range(16):
        counted = counted + jnp.bitwise_and(jnp.right_shift(values, shift_amount), 1)
    return jnp.bitwise_and(counted, 1)


def parity_table(left_bits, right_bits):
    anded = jnp.bitwise_and(left_bits[:, None], right_bits[None, :])
    return 1 - 2 * bit_parity(anded)


def project_rows(inputs, rows_chosen):
    tok_count, feature_width = inputs.shape
    low_size = min(feature_width, 1024)
    high_count = feature_width // low_size
    low_bits = jnp.arange(low_size, dtype=jnp.int32)
    base_table = parity_table(low_bits, rows_chosen).astype(jnp.bfloat16)
    high_bits = jnp.arange(high_count, dtype=jnp.int32) * low_size
    signs_high = parity_table(high_bits, rows_chosen).astype(jnp.float32)
    pieces = inputs.reshape(tok_count, high_count, low_size)
    partial_value = jnp.einsum(
        "thd,dk->thk", pieces, base_table, preferred_element_type=jnp.float32
    )
    return jnp.sum(partial_value * signs_high[None, :, :], axis=1) / math.sqrt(feature_width)


def rank_mix(values, signs):
    rank_size = values.shape[1]
    rank_bits = jnp.arange(rank_size, dtype=jnp.int32)
    table = parity_table(rank_bits, rank_bits).astype(jnp.float32)
    mixed = jnp.dot(
        values * signs, table, precision=lax.Precision.HIGHEST, preferred_element_type=jnp.float32
    )
    return mixed / math.sqrt(rank_size)


def per_device_any_size(
    activations,
    cotangent,
    adapter,
    lengths,
    layout,
    feature_signs,
    rank_signs,
    hadamard_rows,
    entry_pick,
    val_feats,
):
    micro_index = lax.axis_index("batch")
    member = lax.axis_index("fsdp")
    tok_count = activations.shape[1]
    block_count = EX_LEN // tok_count
    example_total = lengths.shape[1]
    slot_row = lax.dynamic_index_in_dim(layout, micro_index, 0, keepdims=False)
    my_slot = lax.dynamic_index_in_dim(slot_row, member, 0, keepdims=False)
    my_example = my_slot // block_count
    length_row = lax.dynamic_index_in_dim(lengths, micro_index, 0, keepdims=False)
    my_length = lax.dynamic_index_in_dim(length_row, my_example, 0, keepdims=False)
    position = my_slot % block_count * tok_count + jnp.arange(tok_count, dtype=jnp.int32)
    weight = (position < my_length).astype(jnp.float32)[:, None]
    inputs = activations[0]
    grads = cotangent[0]
    piece = lax.all_gather(adapter, "fsdp", axis=1, tiled=True)
    reduced = jnp.dot(inputs, piece[0], preferred_element_type=jnp.float32)
    backward = jnp.dot(grads, piece[1], preferred_element_type=jnp.float32)
    signs_in = (1 - 2 * feature_signs[0]).astype(jnp.bfloat16)
    signs_out = (1 - 2 * feature_signs[1]).astype(jnp.bfloat16)
    rank_a = (1 - 2 * rank_signs[0]).astype(jnp.float32)
    rank_b = (1 - 2 * rank_signs[1]).astype(jnp.float32)
    left_a = project_rows(inputs * signs_in[None, :], hadamard_rows[0, :CAND])
    right_b = project_rows(grads * signs_out[None, :], hadamard_rows[1, :CAND])
    right_a = rank_mix(backward, rank_a) * weight
    left_b = rank_mix(reduced, rank_b) * weight
    grid_a = jnp.dot(
        left_a.T, right_a, precision=lax.Precision.HIGHEST, preferred_element_type=jnp.float32
    )
    grid_b = jnp.dot(
        left_b.T, right_b, precision=lax.Precision.HIGHEST, preferred_element_type=jnp.float32
    )
    partial_feats = jnp.concatenate(
        [grid_a.reshape(-1)[entry_pick[0]], grid_b.reshape(-1)[entry_pick[1]]]
    )
    example_ids = jnp.arange(example_total, dtype=jnp.int32)
    mine = (example_ids == my_example).astype(jnp.float32)
    term = mine[:, None] * partial_feats[None, :]
    feat_slice = lax.psum_scatter(term, "fsdp", scatter_dimension=1, tiled=True)
    dots = jnp.dot(
        feat_slice, val_feats.T, precision=lax.Precision.HIGHEST, preferred_element_type=jnp.float32
    )
    feat_sq = jnp.sum(feat_slice * feat_slice, axis=1)
    val_sq = jnp.sum(val_feats * val_feats, axis=1)
    dots, feat_sq, val_sq = lax.psum((dots, feat_sq, val_sq), "fsdp")
    similarity = (
        math.sqrt(K)
        * dots
        * lax.rsqrt(feat_sq[:, None] + 1e-06)
        * lax.rsqrt(val_sq[None, :] + 1e-06)
    )
    return similarity[None]


MESH = pl.DeviceIdType.MESH
F32 = jnp.float32
BF16 = jnp.bfloat16
D_MODEL = 8192
RANK = 128
LOW = 1024
HIGH = D_MODEL // LOW
TOK = 128
MEMBERS = 8
SHARD = D_MODEL // MEMBERS
HALF = K // 2
VALS = 256
SLICE = K // MEMBERS
PLANE_ROWS = 640
CROSS_ROWS = SHARD - PLANE_ROWS


def sign_rows(row, bit):
    signs = (1 - 2 * jnp.bitwise_and(jnp.right_shift(row, bit), 1)).astype(F32)
    return jnp.broadcast_to(signs, (16, row.shape[1])).astype(BF16)


def fill_signs(table_ref, row, bits):
    width = row.shape[1]
    index = lax.broadcasted_iota(jnp.int32, (16, width), 0)
    both = jnp.bitwise_and(index, jnp.broadcast_to(row, (16, width)))
    both = jnp.bitwise_xor(both, jnp.right_shift(both, 2))
    both = jnp.bitwise_xor(both, jnp.right_shift(both, 1))
    table_ref[0:16, :] = (1 - 2 * jnp.bitwise_and(both, 1)).astype(F32).astype(BF16)
    for bit in range(4, bits):
        flip = sign_rows(row, bit)
        span = 1 << bit
        for at in range(0, span, 16):
            table_ref[span + at : span + at + 16, :] = table_ref[at : at + 16, :] * flip


def split_rows(values):
    top = values.astype(BF16)
    rest = (values - top.astype(F32)).astype(BF16)
    return jnp.concatenate([top, rest], axis=0)


def dot_t(left, right):
    return lax.dot_general(
        left, right, (((1,), (1,)), ((), ())), preferred_element_type=F32
    )


def kernel(
    lengths_hbm,
    layout_hbm,
    signs_hbm,
    rank_hbm,
    rows_hbm,
    pick_hbm,
    act_hbm,
    cot_hbm,
    adapter_hbm,
    val_hbm,
    out_ref,
    lengths_ref,
    layout_ref,
    signs_ref,
    rank_ref,
    rows_ref,
    pick_ref,
    act_ref,
    cot_ref,
    val_ref,
    gathered,
    x_ref,
    t_ref,
    left_ref,
    sel_a,
    sel_b,
    mix_a,
    mix_b,
    val_parts,
    val_sq,
    feat_out,
    feat_in,
    dots_out,
    dots_in,
    local_sem,
    z_send,
    z_recv,
    x_send,
    x_recv,
    y_send,
    y_recv,
    ca_send,
    ca_recv,
    cb_send,
    cb_recv,
    f_send,
    f_recv,
    d_send,
    d_recv,
):
    group = lax.axis_index("groups")
    member = lax.axis_index("fsdp")
    core = lax.axis_index("batch")
    col = member % 2
    depth = member // 2
    mates = [
        depth,
        depth + 1 - 2 * (depth % 2),
        2 - depth // 2,
        3 - 3 * (depth // 2),
    ]
    inner = (depth + 1) // 2 % 2 == 1
    other_group = {"groups": 1 - group}
    other_core = {"batch": 1 - core}
    across = {"fsdp": depth * 2 + 1 - col}

    loads = [
        pltpu.make_async_copy(act_hbm.at[0], act_ref, local_sem.at[0]),
        pltpu.make_async_copy(cot_hbm.at[0], cot_ref, local_sem.at[1]),
        pltpu.make_async_copy(val_hbm, val_ref, local_sem.at[2]),
        pltpu.make_async_copy(adapter_hbm.at[0], gathered.at[0, member], local_sem.at[3]),
        pltpu.make_async_copy(adapter_hbm.at[1], gathered.at[1, member], local_sem.at[4]),
        pltpu.make_async_copy(signs_hbm, signs_ref, local_sem.at[5]),
        pltpu.make_async_copy(rank_hbm, rank_ref, local_sem.at[6]),
        pltpu.make_async_copy(rows_hbm, rows_ref, local_sem.at[7]),
        pltpu.make_async_copy(pick_hbm, pick_ref, local_sem.at[8]),
        pltpu.make_async_copy(lengths_hbm, lengths_ref, local_sem.at[9]),
        pltpu.make_async_copy(layout_hbm, layout_ref, local_sem.at[10]),
    ]
    for load in loads[5:] + loads[:5]:
        load.start()

    barrier = pltpu.get_barrier_semaphore()
    for step in range(1, MEMBERS):
        pl.semaphore_signal(
            barrier, inc=1, device_id={"fsdp": (member + step) % MEMBERS}, device_id_type=MESH
        )
    pl.semaphore_signal(barrier, inc=1, device_id=other_group, device_id_type=MESH)
    pl.semaphore_signal(barrier, inc=1, device_id=other_core, device_id_type=MESH)
    pl.semaphore_wait(barrier, MEMBERS + 1)

    plane = pl.ds(pl.multiple_of(group * CROSS_ROWS, 128), PLANE_ROWS)
    cross_out = pl.ds(pl.multiple_of(group * PLANE_ROWS, 128), CROSS_ROWS)
    cross_in = pl.ds(pl.multiple_of((1 - group) * PLANE_ROWS, 128), CROSS_ROWS)
    own = adapter_hbm.at[core, plane]

    def remote(src, dst, send, recv, where):
        return pltpu.make_async_remote_copy(
            src_ref=src,
            dst_ref=dst,
            send_sem=send,
            recv_sem=recv,
            device_id=where,
            device_id_type=MESH,
        )

    sent = []
    sent_inner = []

    def go(copy):
        copy.start()
        sent.append(copy)

    def go_inner(shard, slot, send, to):
        copy = remote(
            slot, gathered.at[core, shard, plane], z_send.at[send[0]], z_recv.at[send[1]],
            {"fsdp": mates[to] * 2 + col},
        )

        @pl.when(inner)
        def _():
            copy.start()

        sent_inner.append(copy)

    home = gathered.at[core, member, plane]
    go(remote(own, home, x_send.at[0], x_recv.at[0], across))
    go(remote(own, home, z_send.at[1], z_recv.at[1], {"fsdp": mates[1] * 2 + col}))
    go_inner(member, own, (2, 2), 2)

    order = [("x", 0), ("z", 1), ("z", 2), ("x", 1), ("z", 3), ("x", 2), ("x", 3)]
    shard_of = [
        mates[k] * 2 + (col if kind == "z" else 1 - col) for kind, k in order
    ]

    def receive(place):
        kind, k = order[place]
        shard = shard_of[place]
        block = gathered.at[core, shard, plane]
        sems = (z_send, z_recv) if kind == "z" else (x_send, x_recv)
        remote(block, block, sems[0].at[k], sems[1].at[k], across).wait_recv()
        if kind == "z":
            if k == 1:
                go_inner(shard, block, (3, 3), 2)
            else:
                go_inner(shard, block, (k + 2, k), 1)
            go(remote(block, block, x_send.at[k], x_recv.at[k], across))
        part = gathered.at[core, shard, cross_out]
        go(remote(part, part, y_send.at[place], y_recv.at[place], other_group))
        go(remote(block, block, ca_send.at[place], ca_recv.at[place], other_core))

    def receive_cross(place):
        part = gathered.at[core, shard_of[place], cross_in]
        remote(part, part, y_send.at[place], y_recv.at[place], other_group).wait_recv()
        go(remote(part, part, cb_send.at[place], cb_recv.at[place], other_core))

    def receive_core(place):
        block = gathered.at[1 - core, shard_of[place], plane]
        part = gathered.at[1 - core, shard_of[place], cross_in]
        remote(block, block, ca_send.at[place], ca_recv.at[place], other_core).wait_recv()
        remote(part, part, cb_send.at[place], cb_recv.at[place], other_core).wait_recv()

    def fill_inputs(which, in_ref):
        for high in range(HIGH):
            lanes = slice(high * LOW, (high + 1) * LOW)
            flip = sign_rows(signs_ref[which : which + 1, lanes], 0)
            for at in range(0, TOK, 16):
                x_ref[high * TOK + at : high * TOK + at + 16, :] = (
                    in_ref[at : at + 16, lanes] * flip
                )

    def project(which, begin, end):
        def tile(n, carry):
            lanes = pl.ds(pl.multiple_of(n * 256, 256), 256)
            parts = jnp.dot(x_ref[...], t_ref[:, lanes], preferred_element_type=F32)
            row = rows_ref[which : which + 1, lanes]
            level = [parts[h * TOK : (h + 1) * TOK] for h in range(HIGH)]
            for bit in range(10, 13):
                flip = (1 - 2 * jnp.bitwise_and(jnp.right_shift(row, bit), 1)).astype(F32)
                level = [
                    level[2 * i] + level[2 * i + 1] * flip for i in range(len(level) // 2)
                ]
            left_ref[:, lanes] = split_rows(level[0])
            return carry

        lax.fori_loop(begin, end, tile, 0)

    def row_index(which, lanes):
        picked = pick_ref[which : which + 1, lanes]
        if which == 0:
            return jnp.right_shift(picked, 7)
        return jnp.bitwise_and(picked, CAND - 1)

    def rank_index(which):
        picked = pick_ref[which : which + 1, :]
        if which == 0:
            return jnp.bitwise_and(picked, RANK - 1)
        return jnp.right_shift(picked, 10)

    def select(which, sel_ref, begin, end):
        def tile(n, carry):
            lanes = pl.ds(pl.multiple_of(n * 256, 256), 256)
            wanted = row_index(which, lanes)
            index = lax.broadcasted_iota(jnp.int32, (CAND, 256), 0)
            hot = jnp.where(index == wanted, 1.0, 0.0).astype(BF16)
            both = jnp.dot(left_ref[...], hot, preferred_element_type=F32)
            sel_ref[:, lanes] = both[:TOK] + both[TOK:]
            return carry

        lax.fori_loop(begin, end, tile, 0)

    def prepare_scores():
        values = val_ref[...]
        val_parts[...] = split_rows(values)
        squares = split_rows(values * values)
        sums = dot_t(jnp.ones((16, SLICE), BF16), squares)
        val_sq[...] = sums[0:8, :VALS] + sums[0:8, VALS:]

    for load in loads[5:]:
        load.wait()
    loads[0].wait()
    fill_signs(t_ref, rows_ref[0:1, 0:CAND], 10)
    receive(0)
    fill_inputs(0, act_ref)
    receive(1)
    project(0, 0, 2)
    receive(2)
    project(0, 2, 4)
    receive(3)
    receive_cross(0)
    select(0, sel_a, 0, 5)
    receive(4)
    receive_cross(1)
    select(0, sel_a, 5, 10)
    receive(5)
    receive_cross(2)
    select(0, sel_a, 10, 16)
    receive(6)
    receive_cross(3)
    loads[1].wait()
    fill_signs(t_ref, rows_ref[1:2, 0:CAND], 10)
    receive_cross(4)
    fill_inputs(1, cot_ref)
    receive_cross(5)
    project(1, 0, 4)
    receive_cross(6)
    select(1, sel_b, 0, 16)
    fill_signs(mix_a, rank_index(0), 7)
    fill_signs(mix_b, rank_index(1), 7)
    loads[2].wait()
    prepare_scores()
    loads[3].wait()
    loads[4].wait()

    def both_products(shard):
        lanes = pl.ds(pl.multiple_of(shard * SHARD, SHARD), SHARD)
        return (
            jnp.dot(act_ref[:, lanes], gathered[0, shard], preferred_element_type=F32),
            jnp.dot(cot_ref[:, lanes], gathered[1, shard], preferred_element_type=F32),
        )

    reduced, backward = both_products(member)
    for place in range(MEMBERS - 1):
        receive_core(place)
        more_r, more_b = both_products(shard_of[place])
        reduced = reduced + more_r
        backward = backward + more_b

    slot = layout_ref[core, member]
    blocks = EX_LEN // TOK
    example = slot // blocks
    length = jnp.int32(0)
    for e in range(lengths_ref.shape[1]):
        length = jnp.where(example == e, lengths_ref[core, e], length)
    position = slot % blocks * TOK + lax.broadcasted_iota(jnp.int32, (TOK, RANK), 0)
    weight = jnp.where(position < length, 1.0, 0.0)
    rank_flip = (1 - 2 * rank_ref[...]).astype(F32)
    mixed_a = split_rows(backward * rank_flip[0:1] * weight)
    mixed_b = split_rows(reduced * rank_flip[1:2] * weight)
    scale = 1.0 / math.sqrt(D_MODEL * RANK)
    for n in range(MEMBERS):
        mixed, mix, sel = (mixed_a, mix_a, sel_a) if n < MEMBERS // 2 else (mixed_b, mix_b, sel_b)
        lanes = slice(n % (MEMBERS // 2) * SLICE, (n % (MEMBERS // 2) + 1) * SLICE)
        both = jnp.dot(mixed, mix[:, lanes], preferred_element_type=F32)
        terms = sel[:, lanes] * (both[:TOK] + both[TOK:])
        feat_out[n] = jnp.sum(terms, axis=0, keepdims=True) * scale

    feat_in[member] = feat_out[member]
    for step in range(1, MEMBERS):
        to = (member + step) % MEMBERS
        go(
            remote(
                feat_out.at[to], feat_in.at[member], f_send.at[step], f_recv.at[step], {"fsdp": to}
            )
        )
    for step in range(1, MEMBERS):
        source = (member + MEMBERS - step) % MEMBERS
        remote(
            feat_out.at[source], feat_in.at[source], f_send.at[step], f_recv.at[step],
            {"fsdp": source},
        ).wait_recv()

    examples = lengths_ref.shape[1]
    totals = [jnp.zeros((1, SLICE), F32) for _ in range(examples)]
    for n in range(MEMBERS):
        owner = layout_ref[core, n] // blocks
        piece = feat_in[n]
        for e in range(examples):
            totals[e] = totals[e] + piece * jnp.where(owner == e, 1.0, 0.0)
    row_at = lax.broadcasted_iota(jnp.int32, (8, SLICE), 0)
    feats = jnp.zeros((8, SLICE), F32)
    for e in range(examples):
        feats = jnp.where(row_at == e, jnp.broadcast_to(totals[e], (8, SLICE)), feats)
    products = dot_t(split_rows(feats), val_parts[...])
    dots = products[0:8, :VALS] + (products[8:16, :VALS] + products[0:8, VALS:])
    feat_sq = jnp.sum(feats * feats, axis=1, keepdims=True)
    at = lax.broadcasted_iota(jnp.int32, (8, VALS), 0)
    dots_out[:, 0:VALS] = jnp.where(at == examples, val_sq[...], dots)
    dots_out[:, VALS:] = jnp.broadcast_to(feat_sq, (8, RANK))
    dots_in[member] = dots_out[...]
    for step in range(1, MEMBERS):
        to = (member + step) % MEMBERS
        go(remote(dots_out, dots_in.at[member], d_send.at[step], d_recv.at[step], {"fsdp": to}))
    for step in range(1, MEMBERS):
        source = (member + MEMBERS - step) % MEMBERS
        remote(
            dots_out, dots_in.at[source], d_send.at[step], d_recv.at[step], {"fsdp": source}
        ).wait_recv()
    total = dots_in[0]
    for n in range(1, MEMBERS):
        total = total + dots_in[n]
    out_ref[0] = (
        math.sqrt(K)
        * total[0:examples, 0:VALS]
        * lax.rsqrt(total[0:examples, VALS : VALS + 1] + 1e-06)
        * lax.rsqrt(total[examples : examples + 1, 0:VALS] + 1e-06)
    )
    for copy in sent:
        copy.wait_send()

    @pl.when(inner)
    def _():
        for copy in sent_inner:
            copy.wait_send()


def per_device(
    activations,
    cotangent,
    adapter,
    lengths,
    layout,
    feature_signs,
    rank_signs,
    hadamard_rows,
    entry_pick,
    val_feats,
):
    examples = lengths.shape[1]
    vmem = pl.BlockSpec(memory_space=pltpu.VMEM)
    hbm = pl.BlockSpec(memory_space=pl.ANY)
    dma = pltpu.SemaphoreType.DMA
    return pl.pallas_call(
        kernel,
        out_shape=jax.ShapeDtypeStruct((1, examples, VALS), F32),
        in_specs=[hbm] * 10,
        out_specs=vmem,
        scratch_shapes=[
            pltpu.SMEM(lengths.shape, jnp.int32),
            pltpu.SMEM(layout.shape, jnp.int32),
            pltpu.VMEM(feature_signs.shape, jnp.int32),
            pltpu.VMEM(rank_signs.shape, jnp.int32),
            pltpu.VMEM(hadamard_rows.shape, jnp.int32),
            pltpu.VMEM(entry_pick.shape, jnp.int32),
            pltpu.VMEM((TOK, D_MODEL), BF16),
            pltpu.VMEM((TOK, D_MODEL), BF16),
            pltpu.VMEM((VALS, SLICE), F32),
            pltpu.VMEM((2, MEMBERS, SHARD, RANK), BF16),
            pltpu.VMEM((HIGH * TOK, LOW), BF16),
            pltpu.VMEM((LOW, CAND), BF16),
            pltpu.VMEM((2 * TOK, CAND), BF16),
            pltpu.VMEM((TOK, HALF), F32),
            pltpu.VMEM((TOK, HALF), F32),
            pltpu.VMEM((RANK, HALF), BF16),
            pltpu.VMEM((RANK, HALF), BF16),
            pltpu.VMEM((2 * VALS, SLICE), BF16),
            pltpu.VMEM((8, VALS), F32),
            pltpu.VMEM((MEMBERS, 1, SLICE), F32),
            pltpu.VMEM((MEMBERS, 1, SLICE), F32),
            pltpu.VMEM((8, VALS + RANK), F32),
            pltpu.VMEM((MEMBERS, 8, VALS + RANK), F32),
            dma((11,)),
        ]
        + [dma((6,))] * 4
        + [dma((MEMBERS,))] * 10,
        compiler_params=pltpu.CompilerParams(
            collective_id=0, has_side_effects=True, vmem_limit_bytes=60 * 1024 * 1024
        ),
        cost_estimate=pl.CostEstimate(
            flops=10_000_000_000, bytes_accessed=8_000_000, transcendentals=0
        ),
    )(
        lengths,
        layout,
        feature_signs,
        rank_signs,
        hadamard_rows,
        entry_pick,
        activations,
        cotangent,
        adapter,
        val_feats,
    )


def solution(mesh):
    fits = mesh.shape["fsdp"] == MEMBERS and mesh.shape["batch"] == 2 and mesh.shape["groups"] == 2
    return jax.shard_map(
        per_device if fits else per_device_any_size,
        mesh=mesh,
        in_specs=(
            P("batch", ("groups", "fsdp"), None),
            P("batch", ("groups", "fsdp"), None),
            P(None, "fsdp", None),
            P(None, "groups"),
            P(None, "groups"),
            P(),
            P(),
            P(),
            P(),
            P("groups", "fsdp"),
        ),
        out_specs=P("batch", "groups", None),
        check_vma=False,
    )
```

```python
import math

import jax
import jax.numpy as jnp
from jax import lax
from jax.experimental import pallas as pl
from jax.experimental.pallas import tpu as pltpu
from jax.sharding import PartitionSpec as P

K = 8192
CAND = 1024
EX_LEN = 512


def bit_parity(values):
    counted = jnp.zeros_like(values)
    for shift_amount in range(16):
        counted = counted + jnp.bitwise_and(jnp.right_shift(values, shift_amount), 1)
    return jnp.bitwise_and(counted, 1)


def parity_table(left_bits, right_bits):
    anded = jnp.bitwise_and(left_bits[:, None], right_bits[None, :])
    return 1 - 2 * bit_parity(anded)


def project_rows(inputs, rows_chosen):
    tok_count, feature_width = inputs.shape
    low_size = min(feature_width, 1024)
    high_count = feature_width // low_size
    low_bits = jnp.arange(low_size, dtype=jnp.int32)
    base_table = parity_table(low_bits, rows_chosen).astype(jnp.bfloat16)
    high_bits = jnp.arange(high_count, dtype=jnp.int32) * low_size
    signs_high = parity_table(high_bits, rows_chosen).astype(jnp.float32)
    pieces = inputs.reshape(tok_count, high_count, low_size)
    partial_value = jnp.einsum(
        "thd,dk->thk", pieces, base_table, preferred_element_type=jnp.float32
    )
    return jnp.sum(partial_value * signs_high[None, :, :], axis=1) / math.sqrt(feature_width)


def rank_mix(values, signs):
    rank_size = values.shape[1]
    rank_bits = jnp.arange(rank_size, dtype=jnp.int32)
    table = parity_table(rank_bits, rank_bits).astype(jnp.float32)
    mixed = jnp.dot(
        values * signs, table, precision=lax.Precision.HIGHEST, preferred_element_type=jnp.float32
    )
    return mixed / math.sqrt(rank_size)


def per_device_any_size(
    activations,
    cotangent,
    adapter,
    lengths,
    layout,
    feature_signs,
    rank_signs,
    hadamard_rows,
    entry_pick,
    val_feats,
):
    micro_index = lax.axis_index("batch")
    member = lax.axis_index("fsdp")
    tok_count = activations.shape[1]
    block_count = EX_LEN // tok_count
    example_total = lengths.shape[1]
    slot_row = lax.dynamic_index_in_dim(layout, micro_index, 0, keepdims=False)
    my_slot = lax.dynamic_index_in_dim(slot_row, member, 0, keepdims=False)
    my_example = my_slot // block_count
    length_row = lax.dynamic_index_in_dim(lengths, micro_index, 0, keepdims=False)
    my_length = lax.dynamic_index_in_dim(length_row, my_example, 0, keepdims=False)
    position = my_slot % block_count * tok_count + jnp.arange(tok_count, dtype=jnp.int32)
    weight = (position < my_length).astype(jnp.float32)[:, None]
    inputs = activations[0]
    grads = cotangent[0]
    piece = lax.all_gather(adapter, "fsdp", axis=1, tiled=True)
    reduced = jnp.dot(inputs, piece[0], preferred_element_type=jnp.float32)
    backward = jnp.dot(grads, piece[1], preferred_element_type=jnp.float32)
    signs_in = (1 - 2 * feature_signs[0]).astype(jnp.bfloat16)
    signs_out = (1 - 2 * feature_signs[1]).astype(jnp.bfloat16)
    rank_a = (1 - 2 * rank_signs[0]).astype(jnp.float32)
    rank_b = (1 - 2 * rank_signs[1]).astype(jnp.float32)
    left_a = project_rows(inputs * signs_in[None, :], hadamard_rows[0, :CAND])
    right_b = project_rows(grads * signs_out[None, :], hadamard_rows[1, :CAND])
    right_a = rank_mix(backward, rank_a) * weight
    left_b = rank_mix(reduced, rank_b) * weight
    grid_a = jnp.dot(
        left_a.T, right_a, precision=lax.Precision.HIGHEST, preferred_element_type=jnp.float32
    )
    grid_b = jnp.dot(
        left_b.T, right_b, precision=lax.Precision.HIGHEST, preferred_element_type=jnp.float32
    )
    partial_feats = jnp.concatenate(
        [grid_a.reshape(-1)[entry_pick[0]], grid_b.reshape(-1)[entry_pick[1]]]
    )
    example_ids = jnp.arange(example_total, dtype=jnp.int32)
    mine = (example_ids == my_example).astype(jnp.float32)
    term = mine[:, None] * partial_feats[None, :]
    feat_slice = lax.psum_scatter(term, "fsdp", scatter_dimension=1, tiled=True)
    dots = jnp.dot(
        feat_slice, val_feats.T, precision=lax.Precision.HIGHEST, preferred_element_type=jnp.float32
    )
    feat_sq = jnp.sum(feat_slice * feat_slice, axis=1)
    val_sq = jnp.sum(val_feats * val_feats, axis=1)
    dots, feat_sq, val_sq = lax.psum((dots, feat_sq, val_sq), "fsdp")
    similarity = (
        math.sqrt(K)
        * dots
        * lax.rsqrt(feat_sq[:, None] + 1e-06)
        * lax.rsqrt(val_sq[None, :] + 1e-06)
    )
    return similarity[None]


MESH = pl.DeviceIdType.MESH
F32 = jnp.float32
BF16 = jnp.bfloat16
D_MODEL = 8192
RANK = 128
LOW = 1024
HIGH = D_MODEL // LOW
TOK = 128
MEMBERS = 8
SHARD = D_MODEL // MEMBERS
HALF = K // 2
VALS = 256
SLICE = K // MEMBERS
PLANE_ROWS = 640
CROSS_ROWS = SHARD - PLANE_ROWS


def sign_rows(row, bit):
    signs = (1 - 2 * jnp.bitwise_and(jnp.right_shift(row, bit), 1)).astype(F32)
    return jnp.broadcast_to(signs, (16, row.shape[1])).astype(BF16)


def fill_signs(table_ref, row, bits):
    width = row.shape[1]
    index = lax.broadcasted_iota(jnp.int32, (16, width), 0)
    both = jnp.bitwise_and(index, jnp.broadcast_to(row, (16, width)))
    both = jnp.bitwise_xor(both, jnp.right_shift(both, 2))
    both = jnp.bitwise_xor(both, jnp.right_shift(both, 1))
    table_ref[0:16, :] = (1 - 2 * jnp.bitwise_and(both, 1)).astype(F32).astype(BF16)
    for bit in range(4, bits):
        flip = sign_rows(row, bit)
        span = 1 << bit
        for at in range(0, span, 16):
            table_ref[span + at : span + at + 16, :] = table_ref[at : at + 16, :] * flip


def split_rows(values):
    top = values.astype(BF16)
    rest = (values - top.astype(F32)).astype(BF16)
    return jnp.concatenate([top, rest], axis=0)


def dot_t(left, right):
    return lax.dot_general(
        left, right, (((1,), (1,)), ((), ())), preferred_element_type=F32
    )


def kernel(
    lengths_hbm,
    layout_hbm,
    signs_hbm,
    rank_hbm,
    rows_hbm,
    pick_hbm,
    act_hbm,
    cot_hbm,
    adapter_hbm,
    val_hbm,
    out_ref,
    lengths_ref,
    layout_ref,
    signs_ref,
    rank_ref,
    rows_ref,
    pick_ref,
    act_ref,
    cot_ref,
    val_ref,
    gathered,
    x_ref,
    t_ref,
    left_ref,
    sel_a,
    sel_b,
    mix_a,
    mix_b,
    val_parts,
    val_sq,
    feat_out,
    feat_in,
    dots_out,
    dots_in,
    local_sem,
    z_send,
    z_recv,
    x_send,
    x_recv,
    y_send,
    y_recv,
    ca_send,
    ca_recv,
    cb_send,
    cb_recv,
    f_send,
    f_recv,
    d_send,
    d_recv,
):
    group = lax.axis_index("groups")
    member = lax.axis_index("fsdp")
    core = lax.axis_index("batch")
    col = member % 2
    depth = member // 2
    mates = [
        depth,
        depth + 1 - 2 * (depth % 2),
        2 - depth // 2,
        3 - 3 * (depth // 2),
    ]
    inner = (depth + 1) // 2 % 2 == 1
    other_group = {"groups": 1 - group}
    other_core = {"batch": 1 - core}
    across = {"fsdp": depth * 2 + 1 - col}

    loads = [
        pltpu.make_async_copy(act_hbm.at[0], act_ref, local_sem.at[0]),
        pltpu.make_async_copy(cot_hbm.at[0], cot_ref, local_sem.at[1]),
        pltpu.make_async_copy(val_hbm, val_ref, local_sem.at[2]),
        pltpu.make_async_copy(adapter_hbm.at[0], gathered.at[0, member], local_sem.at[3]),
        pltpu.make_async_copy(adapter_hbm.at[1], gathered.at[1, member], local_sem.at[4]),
        pltpu.make_async_copy(signs_hbm, signs_ref, local_sem.at[5]),
        pltpu.make_async_copy(rank_hbm, rank_ref, local_sem.at[6]),
        pltpu.make_async_copy(rows_hbm, rows_ref, local_sem.at[7]),
        pltpu.make_async_copy(pick_hbm, pick_ref, local_sem.at[8]),
        pltpu.make_async_copy(lengths_hbm, lengths_ref, local_sem.at[9]),
        pltpu.make_async_copy(layout_hbm, layout_ref, local_sem.at[10]),
    ]
    for load in loads[5:] + loads[:5]:
        load.start()

    barrier = pltpu.get_barrier_semaphore()
    for step in range(1, MEMBERS):
        pl.semaphore_signal(
            barrier, inc=1, device_id={"fsdp": (member + step) % MEMBERS}, device_id_type=MESH
        )
    pl.semaphore_signal(barrier, inc=1, device_id=other_group, device_id_type=MESH)
    pl.semaphore_signal(barrier, inc=1, device_id=other_core, device_id_type=MESH)
    pl.semaphore_wait(barrier, MEMBERS + 1)

    plane = pl.ds(pl.multiple_of(group * CROSS_ROWS, 128), PLANE_ROWS)
    cross_out = pl.ds(pl.multiple_of(group * PLANE_ROWS, 128), CROSS_ROWS)
    cross_in = pl.ds(pl.multiple_of((1 - group) * PLANE_ROWS, 128), CROSS_ROWS)
    own = adapter_hbm.at[core, plane]

    def remote(src, dst, send, recv, where):
        return pltpu.make_async_remote_copy(
            src_ref=src,
            dst_ref=dst,
            send_sem=send,
            recv_sem=recv,
            device_id=where,
            device_id_type=MESH,
        )

    sent = []
    sent_inner = []

    def go(copy):
        copy.start()
        sent.append(copy)

    def go_inner(shard, slot, send, to):
        copy = remote(
            slot, gathered.at[core, shard, plane], z_send.at[send[0]], z_recv.at[send[1]],
            {"fsdp": mates[to] * 2 + col},
        )

        @pl.when(inner)
        def _():
            copy.start()

        sent_inner.append(copy)

    home = gathered.at[core, member, plane]
    go(remote(own, home, x_send.at[0], x_recv.at[0], across))
    go(remote(own, home, z_send.at[1], z_recv.at[1], {"fsdp": mates[1] * 2 + col}))
    go_inner(member, own, (2, 2), 2)

    order = [("x", 0), ("z", 1), ("z", 2), ("x", 1), ("z", 3), ("x", 2), ("x", 3)]
    shard_of = [
        mates[k] * 2 + (col if kind == "z" else 1 - col) for kind, k in order
    ]

    def receive(place):
        kind, k = order[place]
        shard = shard_of[place]
        block = gathered.at[core, shard, plane]
        sems = (z_send, z_recv) if kind == "z" else (x_send, x_recv)
        remote(block, block, sems[0].at[k], sems[1].at[k], across).wait_recv()
        if kind == "z":
            if k == 1:
                go_inner(shard, block, (3, 3), 2)
            else:
                go_inner(shard, block, (k + 2, k), 1)
            go(remote(block, block, x_send.at[k], x_recv.at[k], across))
        part = gathered.at[core, shard, cross_out]
        go(remote(part, part, y_send.at[place], y_recv.at[place], other_group))
        go(remote(block, block, ca_send.at[place], ca_recv.at[place], other_core))

    def receive_cross(place):
        part = gathered.at[core, shard_of[place], cross_in]
        remote(part, part, y_send.at[place], y_recv.at[place], other_group).wait_recv()
        go(remote(part, part, cb_send.at[place], cb_recv.at[place], other_core))

    def receive_core(place):
        block = gathered.at[1 - core, shard_of[place], plane]
        part = gathered.at[1 - core, shard_of[place], cross_in]
        remote(block, block, ca_send.at[place], ca_recv.at[place], other_core).wait_recv()
        remote(part, part, cb_send.at[place], cb_recv.at[place], other_core).wait_recv()

    def fill_inputs(which, in_ref):
        for high in range(HIGH):
            lanes = slice(high * LOW, (high + 1) * LOW)
            flip = sign_rows(signs_ref[which : which + 1, lanes], 0)
            for at in range(0, TOK, 16):
                x_ref[high * TOK + at : high * TOK + at + 16, :] = (
                    in_ref[at : at + 16, lanes] * flip
                )

    def project(which, begin, end):
        def tile(n, carry):
            lanes = pl.ds(pl.multiple_of(n * 256, 256), 256)
            parts = jnp.dot(x_ref[...], t_ref[:, lanes], preferred_element_type=F32)
            row = rows_ref[which : which + 1, lanes]
            level = [parts[h * TOK : (h + 1) * TOK] for h in range(HIGH)]
            for bit in range(10, 13):
                flip = (1 - 2 * jnp.bitwise_and(jnp.right_shift(row, bit), 1)).astype(F32)
                level = [
                    level[2 * i] + level[2 * i + 1] * flip for i in range(len(level) // 2)
                ]
            left_ref[:, lanes] = split_rows(level[0])
            return carry

        lax.fori_loop(begin, end, tile, 0)

    def row_index(which, lanes):
        picked = pick_ref[which : which + 1, lanes]
        if which == 0:
            return jnp.right_shift(picked, 7)
        return jnp.bitwise_and(picked, CAND - 1)

    def rank_index(which):
        picked = pick_ref[which : which + 1, :]
        if which == 0:
            return jnp.bitwise_and(picked, RANK - 1)
        return jnp.right_shift(picked, 10)

    def select(which, sel_ref, begin, end):
        def tile(n, carry):
            lanes = pl.ds(pl.multiple_of(n * 256, 256), 256)
            wanted = row_index(which, lanes)
            index = lax.broadcasted_iota(jnp.int32, (CAND, 256), 0)
            hot = jnp.where(index == wanted, 1.0, 0.0).astype(BF16)
            both = jnp.dot(left_ref[...], hot, preferred_element_type=F32)
            sel_ref[:, lanes] = both[:TOK] + both[TOK:]
            return carry

        lax.fori_loop(begin, end, tile, 0)

    def prepare_scores():
        values = val_ref[...]
        val_parts[...] = split_rows(values)
        squares = split_rows(values * values)
        sums = dot_t(jnp.ones((16, SLICE), BF16), squares)
        val_sq[...] = sums[0:8, :VALS] + sums[0:8, VALS:]

    for load in loads[5:]:
        load.wait()
    loads[0].wait()
    fill_signs(t_ref, rows_ref[0:1, 0:CAND], 10)
    fill_inputs(0, act_ref)
    receive(0)
    receive(1)
    fill_signs(mix_a, rank_index(0), 7)
    fill_signs(mix_b, rank_index(1), 7)
    project(0, 0, 2)
    receive(2)
    loads[2].wait()
    prepare_scores()
    project(0, 2, 4)
    select(0, sel_a, 0, 4)
    receive(3)
    select(0, sel_a, 4, 8)
    receive(4)
    receive_cross(0)
    select(0, sel_a, 8, 12)
    receive(5)
    receive_cross(1)
    select(0, sel_a, 12, 16)
    loads[1].wait()
    fill_signs(t_ref, rows_ref[1:2, 0:CAND], 10)
    receive(6)
    receive_cross(2)
    fill_inputs(1, cot_ref)
    receive_cross(3)
    project(1, 0, 2)
    receive_cross(4)
    project(1, 2, 4)
    receive_cross(5)
    select(1, sel_b, 0, 8)
    receive_cross(6)
    select(1, sel_b, 8, 16)
    loads[3].wait()
    loads[4].wait()

    def both_products(shard):
        lanes = pl.ds(pl.multiple_of(shard * SHARD, SHARD), SHARD)
        return (
            jnp.dot(act_ref[:, lanes], gathered[0, shard], preferred_element_type=F32),
            jnp.dot(cot_ref[:, lanes], gathered[1, shard], preferred_element_type=F32),
        )

    reduced, backward = both_products(member)
    for place in range(MEMBERS - 1):
        receive_core(place)
        more_r, more_b = both_products(shard_of[place])
        reduced = reduced + more_r
        backward = backward + more_b

    slot = layout_ref[core, member]
    blocks = EX_LEN // TOK
    example = slot // blocks
    length = jnp.int32(0)
    for e in range(lengths_ref.shape[1]):
        length = jnp.where(example == e, lengths_ref[core, e], length)
    position = slot % blocks * TOK + lax.broadcasted_iota(jnp.int32, (TOK, RANK), 0)
    weight = jnp.where(position < length, 1.0, 0.0)
    rank_flip = (1 - 2 * rank_ref[...]).astype(F32)
    mixed_a = split_rows(backward * rank_flip[0:1] * weight)
    mixed_b = split_rows(reduced * rank_flip[1:2] * weight)
    scale = 1.0 / math.sqrt(D_MODEL * RANK)
    for n in range(MEMBERS):
        mixed, mix, sel = (mixed_a, mix_a, sel_a) if n < MEMBERS // 2 else (mixed_b, mix_b, sel_b)
        lanes = slice(n % (MEMBERS // 2) * SLICE, (n % (MEMBERS // 2) + 1) * SLICE)
        both = jnp.dot(mixed, mix[:, lanes], preferred_element_type=F32)
        terms = sel[:, lanes] * (both[:TOK] + both[TOK:])
        feat_out[n] = jnp.sum(terms, axis=0, keepdims=True) * scale

    feat_in[member] = feat_out[member]
    for step in range(1, MEMBERS):
        to = (member + step) % MEMBERS
        go(
            remote(
                feat_out.at[to], feat_in.at[member], f_send.at[step], f_recv.at[step], {"fsdp": to}
            )
        )
    for step in range(1, MEMBERS):
        source = (member + MEMBERS - step) % MEMBERS
        remote(
            feat_out.at[source], feat_in.at[source], f_send.at[step], f_recv.at[step],
            {"fsdp": source},
        ).wait_recv()

    examples = lengths_ref.shape[1]
    totals = [jnp.zeros((1, SLICE), F32) for _ in range(examples)]
    for n in range(MEMBERS):
        owner = layout_ref[core, n] // blocks
        piece = feat_in[n]
        for e in range(examples):
            totals[e] = totals[e] + piece * jnp.where(owner == e, 1.0, 0.0)
    row_at = lax.broadcasted_iota(jnp.int32, (8, SLICE), 0)
    feats = jnp.zeros((8, SLICE), F32)
    for e in range(examples):
        feats = jnp.where(row_at == e, jnp.broadcast_to(totals[e], (8, SLICE)), feats)
    products = dot_t(split_rows(feats), val_parts[...])
    dots = products[0:8, :VALS] + (products[8:16, :VALS] + products[0:8, VALS:])
    feat_sq = jnp.sum(feats * feats, axis=1, keepdims=True)
    at = lax.broadcasted_iota(jnp.int32, (8, VALS), 0)
    dots_out[:, 0:VALS] = jnp.where(at == examples, val_sq[...], dots)
    dots_out[:, VALS:] = jnp.broadcast_to(feat_sq, (8, RANK))
    dots_in[member] = dots_out[...]
    for step in range(1, MEMBERS):
        to = (member + step) % MEMBERS
        go(remote(dots_out, dots_in.at[member], d_send.at[step], d_recv.at[step], {"fsdp": to}))
    for step in range(1, MEMBERS):
        source = (member + MEMBERS - step) % MEMBERS
        remote(
            dots_out, dots_in.at[source], d_send.at[step], d_recv.at[step], {"fsdp": source}
        ).wait_recv()
    total = dots_in[0]
    for n in range(1, MEMBERS):
        total = total + dots_in[n]
    out_ref[0] = (
        math.sqrt(K)
        * total[0:examples, 0:VALS]
        * lax.rsqrt(total[0:examples, VALS : VALS + 1] + 1e-06)
        * lax.rsqrt(total[examples : examples + 1, 0:VALS] + 1e-06)
    )
    for copy in sent:
        copy.wait_send()

    @pl.when(inner)
    def _():
        for copy in sent_inner:
            copy.wait_send()


def per_device(
    activations,
    cotangent,
    adapter,
    lengths,
    layout,
    feature_signs,
    rank_signs,
    hadamard_rows,
    entry_pick,
    val_feats,
):
    examples = lengths.shape[1]
    vmem = pl.BlockSpec(memory_space=pltpu.VMEM)
    hbm = pl.BlockSpec(memory_space=pl.ANY)
    dma = pltpu.SemaphoreType.DMA
    return pl.pallas_call(
        kernel,
        out_shape=jax.ShapeDtypeStruct((1, examples, VALS), F32),
        in_specs=[hbm] * 10,
        out_specs=vmem,
        scratch_shapes=[
            pltpu.SMEM(lengths.shape, jnp.int32),
            pltpu.SMEM(layout.shape, jnp.int32),
            pltpu.VMEM(feature_signs.shape, jnp.int32),
            pltpu.VMEM(rank_signs.shape, jnp.int32),
            pltpu.VMEM(hadamard_rows.shape, jnp.int32),
            pltpu.VMEM(entry_pick.shape, jnp.int32),
            pltpu.VMEM((TOK, D_MODEL), BF16),
            pltpu.VMEM((TOK, D_MODEL), BF16),
            pltpu.VMEM((VALS, SLICE), F32),
            pltpu.VMEM((2, MEMBERS, SHARD, RANK), BF16),
            pltpu.VMEM((HIGH * TOK, LOW), BF16),
            pltpu.VMEM((LOW, CAND), BF16),
            pltpu.VMEM((2 * TOK, CAND), BF16),
            pltpu.VMEM((TOK, HALF), F32),
            pltpu.VMEM((TOK, HALF), F32),
            pltpu.VMEM((RANK, HALF), BF16),
            pltpu.VMEM((RANK, HALF), BF16),
            pltpu.VMEM((2 * VALS, SLICE), BF16),
            pltpu.VMEM((8, VALS), F32),
            pltpu.VMEM((MEMBERS, 1, SLICE), F32),
            pltpu.VMEM((MEMBERS, 1, SLICE), F32),
            pltpu.VMEM((8, VALS + RANK), F32),
            pltpu.VMEM((MEMBERS, 8, VALS + RANK), F32),
            dma((11,)),
        ]
        + [dma((6,))] * 4
        + [dma((MEMBERS,))] * 10,
        compiler_params=pltpu.CompilerParams(
            collective_id=0, has_side_effects=True, vmem_limit_bytes=60 * 1024 * 1024
        ),
        cost_estimate=pl.CostEstimate(
            flops=10_000_000_000, bytes_accessed=8_000_000, transcendentals=0
        ),
    )(
        lengths,
        layout,
        feature_signs,
        rank_signs,
        hadamard_rows,
        entry_pick,
        activations,
        cotangent,
        adapter,
        val_feats,
    )


def solution(mesh):
    fits = mesh.shape["fsdp"] == MEMBERS and mesh.shape["batch"] == 2 and mesh.shape["groups"] == 2
    return jax.shard_map(
        per_device if fits else per_device_any_size,
        mesh=mesh,
        in_specs=(
            P("batch", ("groups", "fsdp"), None),
            P("batch", ("groups", "fsdp"), None),
            P(None, "fsdp", None),
            P(None, "groups"),
            P(None, "groups"),
            P(),
            P(),
            P(),
            P(),
            P("groups", "fsdp"),
        ),
        out_specs=P("batch", "groups", None),
        check_vma=False,
    )
```
